32 devices in a mesh: item: 8 (over y, x, core), split: 4 (over z).
Axes of the slice: x: 2, y: 2, z: 4, core: 2. Of those that a mesh axis runs over, the one named last changes fastest.
Arguments:
- item_emb: float32 [4096, 128], P('item'), may hold values from -0.09375 to 0.09375
- confidences: bfloat16 [8, 4, 4, 16, 8, 128], P('item', 'split'), may hold values from 1 to 64
- user_block: int32 [8, 4, 4, 16], P('item', 'split'), may hold values from 0 to 2
- item_block: int32 [8, 4, 4, 16], P('item', 'split'), may hold values from 0 to 3
- block_age: int32 [8, 4, 4, 16], P('item', 'split'), may hold values from 0 to 15
- block_count: int32 [8, 4, 4], P('item', 'split'), may hold values from 8 to 16, as said below
Outputs:
- user_emb: float32 [192, 128], P('item')
The draws below stay inside these ranges and needn't reach their ends.
Inputs may be any that keep to these rules, and one draw needn't show every extreme that they name: `block_count`: every device has 16 live slots at some window offset in some draw; some device has them in every draw.
All inputs are finite; a program needn't handle non-finite values.
Results may differ from the reference program's by a relative error of at most 0.0003.
Values sent between devices are 32-bit elements; how exact they have to be, the bound alone decides.
No kernel may reach another device: no remote copies, remote signals or barrier semaphores. Data moves between devices by JAX's collectives and lax.ppermute only.
A program may use at most 64 MiB of HBM per device.

```python
import math
import jax
import jax.numpy as jnp
from jax import lax

EMB = 128
BLOCK_ITEMS = 128
BLOCK_USERS = 8
USER_BLOCKS = 3
ITEM_BLOCKS = 4
BLK_STEP = 16
STEPS = 4
CG_ITERS = 3
ITEM_ROWS = 512
ITEMS = 4096
USERS_DEV = 24
USERS = 192
N_ITEM = 8
N_SPLIT = 4


def draw_block_count(key, part):
    key_drop, key_chosen = jax.random.split(key, 2)
    drop = jax.random.randint(key_drop, (N_ITEM, N_SPLIT, STEPS), 0, max(2, BLK_STEP // 2 + 1))
    counts = BLK_STEP - drop
    chosen = jax.random.randint(key_chosen, (), 0, N_ITEM * N_SPLIT * STEPS)
    flattened = counts.reshape(-1).at[chosen].set(BLK_STEP)
    return flattened.reshape(N_ITEM, N_SPLIT, STEPS).astype(jnp.int32)


def with_ends(drawn, stream_key, low, high):
    extent = drawn.shape
    index_at = [jax.random.randint(jax.random.fold_in(stream_key, axis), (), 0, extent[axis]) for axis in range(len(extent))]
    drawn = drawn.at[tuple(index_at)].set(low)
    longest = extent.index(max(extent))
    index_at[longest] = (index_at[longest] + 1) % extent[longest]
    return drawn.at[tuple(index_at)].set(high)


def level_of(rng, dims, shards, low, top_value):
    gain = 1.0
    for axis_at, blocks in shards:
        draws = jax.random.uniform(jax.random.fold_in(jax.random.fold_in(rng, 6), axis_at), (blocks,), jnp.float32, low / len(shards), top_value / len(shards))
        gain = gain * jnp.repeat(jnp.exp(draws), dims[axis_at] // blocks).reshape((-1,) + (1,) * (len(dims) - 1 - axis_at))
    return gain


def normal_values(key, extent, scale, reach, cuts=(), kind=jnp.bfloat16):
    array = scale * jax.random.normal(key, extent, jnp.float32)
    if cuts:
        array = array * level_of(key, extent, cuts, -0.22, 0.18)
    return jnp.clip(array, -reach, reach).astype(kind)


def setup_inputs(seed: int = 0) -> dict:
    arg_keys = jax.random.split(jax.random.key(seed), 7)
    return {
        "item_emb": normal_values(arg_keys[0], (ITEMS, EMB), ITEMS ** -0.5, 0.09375, ((0, 8),), jnp.float32),
        "confidences": jnp.clip(jnp.exp(math.log(64.0) - 4.158883 * jax.random.uniform(arg_keys[1], (N_ITEM, N_SPLIT, STEPS, BLK_STEP, BLOCK_USERS, BLOCK_ITEMS), jnp.float32) ** level_of(arg_keys[1], (N_ITEM, N_SPLIT, STEPS, BLK_STEP, BLOCK_USERS, BLOCK_ITEMS), ((0, 8), (1, 4)), -0.2, 0.2)), 1.0, 64.0).astype(jnp.bfloat16),
        "user_block": with_ends(jax.random.randint(arg_keys[2], (N_ITEM, N_SPLIT, STEPS, BLK_STEP), 0, USER_BLOCKS), jax.random.fold_in(arg_keys[2], 1), 0, USER_BLOCKS - 1).astype(jnp.int32),
        "item_block": with_ends(jax.random.randint(arg_keys[3], (N_ITEM, N_SPLIT, STEPS, BLK_STEP), 0, ITEM_BLOCKS), jax.random.fold_in(arg_keys[3], 1), 0, ITEM_BLOCKS - 1).astype(jnp.int32),
        "block_age": with_ends(jax.random.randint(arg_keys[4], (N_ITEM, N_SPLIT, STEPS, BLK_STEP), 0, 16), jax.random.fold_in(arg_keys[4], 1), 0, 15).astype(jnp.int32),
        "block_count": draw_block_count(jax.random.fold_in(arg_keys[6], 71), 0),
    }


ridge_weight = 0.1


def conjugate(matrix, right):
    solution = jnp.zeros_like(right)
    residual = right
    direction = right
    norm_now = jnp.sum(residual * residual, axis=1)
    for iteration in range(CG_ITERS):
        image = jnp.einsum('ude,ue->ud', matrix, direction, precision=lax.Precision.HIGHEST)
        step_size = norm_now / jnp.sum(direction * image, axis=1)
        solution = solution + step_size[:, None] * direction
        residual = residual - step_size[:, None] * image
        norm_next = jnp.sum(residual * residual, axis=1)
        direction = residual + (norm_next / norm_now)[:, None] * direction
        norm_now = norm_next
    return solution


def reference(item_emb, confidences, user_block, item_block, block_age, block_count):
    base = jnp.dot(item_emb.T, item_emb, precision=lax.Precision.HIGHEST, preferred_element_type=jnp.float32)
    base = base + ridge_weight * jnp.eye(EMB, dtype=jnp.float32)

    def solve_group(group):
        window = jnp.concatenate([lax.dynamic_slice_in_dim(item_emb, (((group - offset) % N_ITEM) * ITEM_ROWS).astype(jnp.int32), ITEM_ROWS, 0) for offset in range(STEPS)], axis=0)
        weights = lax.dynamic_index_in_dim(confidences, group, 0, keepdims=False).astype(jnp.float32)
        users_here = lax.dynamic_index_in_dim(user_block, group, 0, keepdims=False)
        items_here = lax.dynamic_index_in_dim(item_block, group, 0, keepdims=False)
        ages_here = lax.dynamic_index_in_dim(block_age, group, 0, keepdims=False)
        counts_here = lax.dynamic_index_in_dim(block_count, group, 0, keepdims=False)
        recency = 2.0 / (2.0 + ages_here.astype(jnp.float32))
        live = (jnp.arange(BLK_STEP, dtype=jnp.int32)[None, None, :] < counts_here[:, :, None]).astype(jnp.float32)
        factor = (recency * live)[..., None, None]
        conf_part = weights * factor
        pref_part = (weights + 1.0) * factor
        row_index = users_here[..., None, None] * BLOCK_USERS + jnp.arange(BLOCK_USERS, dtype=jnp.int32)[:, None]
        col_index = jnp.arange(STEPS, dtype=jnp.int32)[None, :, None, None, None] * ITEM_ROWS + items_here[..., None, None] * BLOCK_ITEMS + jnp.arange(BLOCK_ITEMS, dtype=jnp.int32)[None, :]
        row_index = jnp.broadcast_to(row_index, conf_part.shape)
        col_index = jnp.broadcast_to(col_index, conf_part.shape)
        conf_weight = jnp.zeros((USERS_DEV, STEPS * ITEM_ROWS), jnp.float32).at[row_index, col_index].add(conf_part)
        pref_weight = jnp.zeros((USERS_DEV, STEPS * ITEM_ROWS), jnp.float32).at[row_index, col_index].add(pref_part)
        system = jnp.einsum('ui,id,ie->ude', conf_weight, window, window, precision=lax.Precision.HIGHEST) + base[None]
        right = jnp.dot(pref_weight, window, precision=lax.Precision.HIGHEST, preferred_element_type=jnp.float32)
        return conjugate(system, right)

    solved = lax.map(solve_group, jnp.arange(N_ITEM, dtype=jnp.int32))
    return solved.reshape(USERS, EMB)
```

```python
import functools

import jax
import jax.numpy as jnp
from jax import lax
from jax.experimental import pallas as pl
from jax.experimental.pallas import tpu as pltpu
from jax.sharding import PartitionSpec as P

USER_BLOCKS = 3
STEPS = 4
CG_ITERS = 3
RIDGE = 0.1

SUB = 8
LANES = 128


def split_parts(value):
    high = value.astype(jnp.bfloat16).astype(jnp.float32)
    return high, value - high


def prepare_kernel(n_split, item_blocks, conf_tiles, gram_tiles, users, items, ages, counts, conf, emb, *rest):
    sends, gram_out, acc, gram = rest[:n_split], rest[n_split], rest[n_split + 1], rest[n_split + 2]
    cells = STEPS * item_blocks
    slots = conf.shape[3]
    z = lax.axis_index("split")
    odd = lax.rem(lax.axis_index("item"), 2)
    acc[...] = jnp.zeros_like(acc)
    lane = lax.broadcasted_iota(jnp.int32, (SUB, LANES), 1)
    recency_sums = jnp.zeros((SUB, LANES), jnp.float32)
    for k in range(STEPS):
        place = jnp.where(odd == 1, k, (STEPS - k) % STEPS)
        for j in range(slots):
            tile = users[0, 0, k, j] * cells + place * item_blocks + items[0, 0, k, j]
            age = jnp.full((SUB, LANES), ages[0, 0, k, j], jnp.int32).astype(jnp.float32)
            live = (j < counts[0, 0, k]).astype(jnp.float32)
            recency = 2.0 / (2.0 + age) * live
            acc[tile] = acc[tile] + conf[0, 0, k, j].astype(jnp.float32) * recency
            recency_sums = recency_sums + jnp.where(lane == tile, recency, 0.0)
    acc[USER_BLOCKS * cells] = recency_sums
    for s in range(n_split):
        chunk = lax.rem(z + s, n_split)
        sends[s][...] = acc[pl.ds(chunk * conf_tiles, conf_tiles)]

    value = emb[...]
    gram[...] = jnp.zeros_like(gram)
    product = lax.dot_general(
        value, value, (((0,), (0,)), ((), ())), precision=lax.Precision.HIGHEST, preferred_element_type=jnp.float32
    )
    gram[0 : LANES // SUB] = product.reshape(LANES // SUB, SUB, LANES)
    gram_out[...] = gram[pl.ds(z * gram_tiles, gram_tiles)]


def solve_kernel(n_split, item_blocks, conf_tiles, gram_tiles, *refs):
    shards = refs[:STEPS]
    chunks = refs[STEPS : STEPS + n_split]
    out, weights, gram, wide, tall = refs[STEPS + n_split :]
    cells = STEPS * item_blocks
    z = lax.axis_index("split")
    rows = shards[0].shape[0]
    users = USER_BLOCKS * SUB
    features = LANES

    for s in range(n_split):
        chunk = lax.rem(z + n_split - s, n_split)
        weights[pl.ds(chunk * conf_tiles, conf_tiles)] = chunks[s][0:conf_tiles]
        gram[pl.ds(chunk * gram_tiles, gram_tiles)] = chunks[s][conf_tiles : conf_tiles + gram_tiles]

    for k in range(STEPS):
        high, low = split_parts(shards[k][...])
        tall[k] = jnp.concatenate([high, low], axis=1).astype(jnp.bfloat16)
        wide[k] = jnp.concatenate([high.T, low.T], axis=0).astype(jnp.bfloat16)

    eye_rows = lax.broadcasted_iota(jnp.int32, (features, features), 0)
    eye_cols = lax.broadcasted_iota(jnp.int32, (features, features), 1)
    base = gram[0 : features // SUB].reshape(features, features) + jnp.where(eye_rows == eye_cols, RIDGE, 0.0)
    base_high, base_low = split_parts(base)
    base_pair = jnp.concatenate([base_high, base_low], axis=1).astype(jnp.bfloat16)

    def conf_of(k):
        return jnp.concatenate(
            [
                jnp.concatenate([weights[ub * cells + k * item_blocks + i] for i in range(item_blocks)], axis=1)
                for ub in range(USER_BLOCKS)
            ],
            axis=0,
        )

    recency_sums = weights[USER_BLOCKS * cells]

    def count_of(k):
        return jnp.concatenate(
            [
                jnp.concatenate(
                    [
                        jnp.broadcast_to(recency_sums[:, t : t + 1], (SUB, LANES))
                        for t in range(ub * cells + k * item_blocks, ub * cells + (k + 1) * item_blocks)
                    ],
                    axis=1,
                )
                for ub in range(USER_BLOCKS)
            ],
            axis=0,
        )

    def stacked(value):
        high, low = split_parts(value)
        return jnp.concatenate([high, low], axis=0).astype(jnp.bfloat16)

    def folded(pair):
        return (pair[:users, :features] + pair[:users, features:]) + (pair[users:, :features] + pair[users:, features:])

    def back(value, k):
        return jnp.dot(stacked(value), tall[k], preferred_element_type=jnp.float32)

    right = folded(sum(back(conf_of(k) + count_of(k), k) for k in range(STEPS)))

    def apply(direction):
        high, low = split_parts(direction)
        left = jnp.concatenate(
            [jnp.concatenate([high, high], axis=1), jnp.concatenate([low, low], axis=1)], axis=0
        ).astype(jnp.bfloat16)
        total = jnp.dot(left[:, :features], base_pair, preferred_element_type=jnp.float32)
        for k in range(STEPS):
            scores = jnp.dot(left, wide[k], preferred_element_type=jnp.float32)
            total = total + back((scores[:users] + scores[users:]) * conf_of(k), k)
        return folded(total)

    answer = jnp.zeros_like(right)
    residual = right
    direction = right
    norm_now = jnp.sum(residual * residual, axis=1, keepdims=True)
    for iteration in range(CG_ITERS):
        image = apply(direction)
        step = norm_now / jnp.sum(direction * image, axis=1, keepdims=True)
        answer = answer + step * direction
        if iteration + 1 < CG_ITERS:
            residual = residual - step * image
            norm_next = jnp.sum(residual * residual, axis=1, keepdims=True)
            direction = residual + (norm_next / norm_now) * direction
            norm_now = norm_next
    out[...] = answer


def body(item_emb, confidences, user_block, item_block, block_age, block_count):
    n_item, n_split = lax.axis_size("item"), lax.axis_size("split")
    rows, features = item_emb.shape
    block_users, block_items = confidences.shape[4:]
    item_blocks = rows // block_items
    tiles = USER_BLOCKS * STEPS * item_blocks + 1
    conf_tiles = pl.cdiv(tiles, n_split)
    gram_tiles = pl.cdiv(features // SUB, n_split)
    f32 = jnp.float32
    smem = pl.BlockSpec(memory_space=pltpu.SMEM)
    vmem = pl.BlockSpec(memory_space=pltpu.VMEM)

    def over_split(value, steps):
        return lax.ppermute(value, "split", [(i, (i + steps) % n_split) for i in range(n_split)])

    second = lax.ppermute(item_emb, "item", [(i, (i + 2) % n_item) for i in range(n_item)])
    first = lax.ppermute(item_emb, "item", [(i, (i + (3 if i % 2 else 1)) % n_item) for i in range(n_item)])
    third = lax.ppermute(second, "item", [(i, i ^ 1) for i in range(n_item)])

    prepared = pl.pallas_call(
        functools.partial(prepare_kernel, n_split, item_blocks, conf_tiles, gram_tiles),
        out_shape=[jax.ShapeDtypeStruct((conf_tiles, SUB, LANES), f32)] * n_split
        + [jax.ShapeDtypeStruct((gram_tiles, SUB, LANES), f32)],
        in_specs=[smem] * 4 + [vmem] * 2,
        out_specs=[vmem] * (n_split + 1),
        scratch_shapes=[
            pltpu.VMEM((n_split * conf_tiles, SUB, LANES), f32),
            pltpu.VMEM((n_split * gram_tiles, SUB, LANES), f32),
        ],
        name="prepare",
    )(user_block, item_block, block_age, block_count, confidences, item_emb)
    sends, gram = prepared[:n_split], prepared[n_split]

    distance = 1
    while distance < n_item:
        gram = gram + lax.ppermute(gram, "item", [(i, i ^ distance) for i in range(n_item)])
        distance *= 2
    mine = sends[0]
    for s in range(1, n_split):
        mine = mine + over_split(sends[s], s)
    mine = jnp.concatenate([mine, gram], axis=0)
    chunks = [mine] + [over_split(mine, s) for s in range(1, n_split)]

    return pl.pallas_call(
        functools.partial(solve_kernel, n_split, item_blocks, conf_tiles, gram_tiles),
        out_shape=jax.ShapeDtypeStruct((USER_BLOCKS * block_users, features), f32),
        in_specs=[vmem] * (STEPS + n_split),
        out_specs=vmem,
        scratch_shapes=[
            pltpu.VMEM((n_split * conf_tiles, SUB, LANES), f32),
            pltpu.VMEM((n_split * gram_tiles, SUB, LANES), f32),
            pltpu.VMEM((STEPS, 2 * features, rows), jnp.bfloat16),
            pltpu.VMEM((STEPS, rows, 2 * features), jnp.bfloat16),
        ],
        name="solve",
    )(item_emb, first, second, third, *chunks)


def solution(mesh):
    placed = (
        P("item", None),
        P("item", "split", None, None, None, None),
        P("item", "split", None, None),
        P("item", "split", None, None),
        P("item", "split", None, None),
        P("item", "split", None),
    )
    return jax.shard_map(
        body, mesh=mesh, in_specs=placed, out_specs=P("item", None), check_vma=False
    )
```

```python
import functools

import jax
import jax.numpy as jnp
from jax import lax
from jax.experimental import pallas as pl
from jax.experimental.pallas import tpu as pltpu
from jax.sharding import PartitionSpec as P

USER_BLOCKS = 3
STEPS = 4
CG_ITERS = 3
RIDGE = 0.1
VMEM_LIMIT = 16 * 2**20

SUB = 8
LANES = 128


def split_parts(value):
    high = value.astype(jnp.bfloat16).astype(jnp.float32)
    return high, value - high


def weights_kernel(item_blocks, half, *refs):
    arrays, (keep, send), held, (acc, arrived) = refs[:5], refs[5:7], refs[7:12], refs[12:]
    copies = [pltpu.make_async_copy(a, h, arrived.at[i]) for i, (a, h) in enumerate(zip(arrays, held))]
    for copy in copies:
        copy.start()
    acc[...] = jnp.zeros_like(acc)
    for copy in copies:
        copy.wait()
    users, items, ages, counts, conf = held
    cells = STEPS * item_blocks
    slots = conf.shape[3]
    upper = lax.rem(lax.axis_index("split"), 2)
    odd = lax.rem(lax.axis_index("item"), 2)
    lane = lax.broadcasted_iota(jnp.int32, (SUB, LANES), 1)
    recency_sums = jnp.zeros((SUB, LANES), jnp.float32)
    for k in range(STEPS):
        place = jnp.where(odd == 1, k, (STEPS - k) % STEPS)
        for j in range(slots):
            tile = users[0, 0, k, j] * cells + place * item_blocks + items[0, 0, k, j]
            age = jnp.full((SUB, LANES), ages[0, 0, k, j], jnp.int32).astype(jnp.float32)
            live = (j < counts[0, 0, k]).astype(jnp.float32)
            recency = 2.0 / (2.0 + age) * live
            acc[tile] = acc[tile] + conf[0, 0, k, j].astype(jnp.float32) * recency
            recency_sums = recency_sums + jnp.where(lane == tile, recency, 0.0)
    acc[USER_BLOCKS * cells] = recency_sums
    keep[...] = acc[pl.ds(upper * half, half)]
    send[...] = acc[pl.ds((1 - upper) * half, half)]


def gram_kernel(emb, out):
    value = emb[...]
    out[...] = lax.dot_general(
        value, value, (((0,), (0,)), ((), ())), precision=lax.Precision.HIGHEST, preferred_element_type=jnp.float32
    )


def solve_kernel(item_blocks, half, *refs):
    shards = refs[:STEPS]
    gram, keep, other, out, weights, wide, tall = refs[STEPS:]
    cells = STEPS * item_blocks
    upper = lax.rem(lax.axis_index("split"), 2)
    users = USER_BLOCKS * SUB
    features = LANES

    weights[pl.ds(upper * half, half)] = keep[...]
    weights[pl.ds((1 - upper) * half, half)] = other[...]

    for k in range(STEPS):
        high, low = split_parts(shards[k][...])
        tall[k] = jnp.concatenate([high, low], axis=1).astype(jnp.bfloat16)
        wide[k] = jnp.concatenate([high.T, low.T], axis=0).astype(jnp.bfloat16)

    eye_rows = lax.broadcasted_iota(jnp.int32, (features, features), 0)
    eye_cols = lax.broadcasted_iota(jnp.int32, (features, features), 1)
    base = gram[...] + jnp.where(eye_rows == eye_cols, RIDGE, 0.0)
    base_high, base_low = split_parts(base)
    base_pair = jnp.concatenate([base_high, base_low], axis=1).astype(jnp.bfloat16)

    def conf_of(k):
        return jnp.concatenate(
            [
                jnp.concatenate([weights[ub * cells + k * item_blocks + i] for i in range(item_blocks)], axis=1)
                for ub in range(USER_BLOCKS)
            ],
            axis=0,
        )

    recency_sums = weights[USER_BLOCKS * cells]

    def count_of(k):
        return jnp.concatenate(
            [
                jnp.concatenate(
                    [
                        jnp.broadcast_to(recency_sums[:, t : t + 1], (SUB, LANES))
                        for t in range(ub * cells + k * item_blocks, ub * cells + (k + 1) * item_blocks)
                    ],
                    axis=1,
                )
                for ub in range(USER_BLOCKS)
            ],
            axis=0,
        )

    def stacked(value):
        high, low = split_parts(value)
        return jnp.concatenate([high, low], axis=0).astype(jnp.bfloat16)

    def folded(pair):
        return (pair[:users, :features] + pair[:users, features:]) + (pair[users:, :features] + pair[users:, features:])

    def back(value, k):
        return jnp.dot(stacked(value), tall[k], preferred_element_type=jnp.float32)

    right = folded(sum(back(conf_of(k) + count_of(k), k) for k in range(STEPS)))

    def apply(direction):
        high, low = split_parts(direction)
        left = jnp.concatenate(
            [jnp.concatenate([high, high], axis=1), jnp.concatenate([low, low], axis=1)], axis=0
        ).astype(jnp.bfloat16)
        total = jnp.dot(left[:, :features], base_pair, preferred_element_type=jnp.float32)
        for k in range(STEPS):
            scores = jnp.dot(left, wide[k], preferred_element_type=jnp.float32)
            total = total + back((scores[:users] + scores[users:]) * conf_of(k), k)
        return folded(total)

    answer = jnp.zeros_like(right)
    residual = right
    direction = right
    norm_now = jnp.sum(residual * residual, axis=1, keepdims=True)
    for iteration in range(CG_ITERS):
        image = apply(direction)
        step = norm_now / jnp.sum(direction * image, axis=1, keepdims=True)
        answer = answer + step * direction
        if iteration + 1 < CG_ITERS:
            residual = residual - step * image
            norm_next = jnp.sum(residual * residual, axis=1, keepdims=True)
            direction = residual + (norm_next / norm_now) * direction
            norm_now = norm_next
    out[...] = answer


def body(item_emb, confidences, user_block, item_block, block_age, block_count):
    n_item, n_split = lax.axis_size("item"), lax.axis_size("split")
    rows, features = item_emb.shape
    block_users, block_items = confidences.shape[4:]
    item_blocks = rows // block_items
    half = pl.cdiv(USER_BLOCKS * STEPS * item_blocks + 1, 2)
    f32 = jnp.float32
    hbm = pl.BlockSpec(memory_space=pltpu.HBM)
    vmem = pl.BlockSpec(memory_space=pltpu.VMEM)
    params = pltpu.CompilerParams(vmem_limit_bytes=VMEM_LIMIT)
    half_tiles = jax.ShapeDtypeStruct((half, SUB, LANES), f32)

    def pair(value, axis):
        return lax.ppermute(value, axis, [(i, i ^ 1) for i in range(lax.axis_size(axis))])

    def shifted(value, axis, steps):
        count = lax.axis_size(axis)
        return lax.ppermute(value, axis, [(i, (i + steps) % count) for i in range(count)])

    slot_arrays = (user_block, item_block, block_age, block_count)
    keep, send = pl.pallas_call(
        functools.partial(weights_kernel, item_blocks, half),
        out_shape=[half_tiles, half_tiles],
        in_specs=[hbm] * 5,
        out_specs=[vmem] * 2,
        scratch_shapes=[pltpu.SMEM(a.shape, a.dtype) for a in slot_arrays]
        + [
            pltpu.VMEM(confidences.shape, confidences.dtype),
            pltpu.VMEM((2 * half, SUB, LANES), f32),
            pltpu.SemaphoreType.DMA((5,)),
        ],
        compiler_params=params,
        name="weights",
    )(*[pltpu.with_memory_space_constraint(a, pltpu.HBM) for a in (*slot_arrays, confidences)])
    keep = keep + pair(send, "split")

    second, sent = lax.optimization_barrier((shifted(item_emb, "item", 2), item_emb))
    first = lax.ppermute(sent, "item", [(i, (i + (3 if i % 2 else 1)) % n_item) for i in range(n_item)])
    third = pair(second, "item")

    gram = pl.pallas_call(
        gram_kernel,
        out_shape=jax.ShapeDtypeStruct((features, features), f32),
        in_specs=[vmem],
        out_specs=vmem,
        compiler_params=params,
        name="gram",
    )(item_emb)
    chip_gram = gram + pair(gram, "item")
    keep, chip_gram = lax.optimization_barrier((keep, chip_gram))
    gram = chip_gram
    for steps in range(2, n_item, 2):
        gram = gram + shifted(chip_gram, "item", steps)

    total = keep
    for steps in range(2, n_split, 2):
        total = total + shifted(keep, "split", steps)
    other = pair(total, "split")

    return pl.pallas_call(
        functools.partial(solve_kernel, item_blocks, half),
        out_shape=jax.ShapeDtypeStruct((USER_BLOCKS * block_users, features), f32),
        in_specs=[vmem] * (STEPS + 3),
        out_specs=vmem,
        scratch_shapes=[
            pltpu.VMEM((2 * half, SUB, LANES), f32),
            pltpu.VMEM((STEPS, 2 * features, rows), jnp.bfloat16),
            pltpu.VMEM((STEPS, rows, 2 * features), jnp.bfloat16),
        ],
        compiler_params=params,
        name="solve",
    )(item_emb, first, second, third, gram, total, other)


def solution(mesh):
    placed = (
        P("item", None),
        P("item", "split", None, None, None, None),
        P("item", "split", None, None),
        P("item", "split", None, None),
        P("item", "split", None, None),
        P("item", "split", None),
    )
    return jax.shard_map(
        body, mesh=mesh, in_specs=placed, out_specs=P("item", None), check_vma=False
    )
```

```python
import functools

import jax
import jax.numpy as jnp
from jax import lax
from jax.experimental import pallas as pl
from jax.experimental.pallas import tpu as pltpu
from jax.sharding import PartitionSpec as P

USER_BLOCKS = 3
STEPS = 4
CG_ITERS = 3
RIDGE = 0.1
VMEM_LIMIT = 16 * 2**20

SUB = 8
LANES = 128


def split_parts(value):
    high = value.astype(jnp.bfloat16).astype(jnp.float32)
    return high, value - high


def weights_kernel(item_blocks, half, *refs):
    arrays, (keep, send), held, (acc, arrived) = refs[:5], refs[5:7], refs[7:12], refs[12:]
    copies = [pltpu.make_async_copy(a, h, arrived.at[i]) for i, (a, h) in enumerate(zip(arrays, held))]
    for copy in copies:
        copy.start()
    acc[...] = jnp.zeros_like(acc)
    for copy in copies:
        copy.wait()
    users, items, ages, counts, conf = held
    cells = STEPS * item_blocks
    slots = conf.shape[3]
    upper = lax.rem(lax.axis_index("split"), 2)
    odd = lax.rem(lax.axis_index("item"), 2)
    lane = lax.broadcasted_iota(jnp.int32, (SUB, LANES), 1)
    recency_sums = jnp.zeros((SUB, LANES), jnp.float32)
    for k in range(STEPS):
        place = jnp.where(odd == 1, k, (STEPS - k) % STEPS)
        for j in range(slots):
            tile = users[0, 0, k, j] * cells + place * item_blocks + items[0, 0, k, j]
            age = jnp.full((SUB, LANES), ages[0, 0, k, j], jnp.int32).astype(jnp.float32)
            live = (j < counts[0, 0, k]).astype(jnp.float32)
            recency = 2.0 / (2.0 + age) * live
            acc[tile] = acc[tile] + conf[0, 0, k, j].astype(jnp.float32) * recency
            recency_sums = recency_sums + jnp.where(lane == tile, recency, 0.0)
    acc[USER_BLOCKS * cells] = recency_sums
    keep[...] = acc[pl.ds(upper * half, half)]
    send[...] = acc[pl.ds((1 - upper) * half, half)]


def gram_kernel(emb, second, out):
    total = 0.0
    for shard in (emb, second):
        high, low = split_parts(shard[...])
        upright = jnp.concatenate([high, low], axis=1).astype(jnp.bfloat16)
        across = jnp.concatenate([high.T, low.T], axis=0).astype(jnp.bfloat16)
        total = total + jnp.dot(across, upright, preferred_element_type=jnp.float32)
    total = total[:LANES] + total[LANES:]
    out[...] = total[:, :LANES] + total[:, LANES:]


def solve_kernel(item_blocks, half, *refs):
    shards = refs[:STEPS]
    gram, keep, other, out, weights, wide, tall = refs[STEPS:]
    cells = STEPS * item_blocks
    upper = lax.rem(lax.axis_index("split"), 2)
    users = USER_BLOCKS * SUB
    features = LANES

    weights[pl.ds(upper * half, half)] = keep[...]
    weights[pl.ds((1 - upper) * half, half)] = other[...]

    for k in range(STEPS):
        high, low = split_parts(shards[k][...])
        tall[k] = jnp.concatenate([high, low], axis=1).astype(jnp.bfloat16)
        wide[k] = jnp.concatenate([high.T, low.T], axis=0).astype(jnp.bfloat16)

    eye_rows = lax.broadcasted_iota(jnp.int32, (features, features), 0)
    eye_cols = lax.broadcasted_iota(jnp.int32, (features, features), 1)
    base = gram[...] + jnp.where(eye_rows == eye_cols, RIDGE, 0.0)
    base_high, base_low = split_parts(base)
    base_pair = jnp.concatenate([base_high, base_low], axis=1).astype(jnp.bfloat16)

    def conf_of(k):
        return jnp.concatenate(
            [
                jnp.concatenate([weights[ub * cells + k * item_blocks + i] for i in range(item_blocks)], axis=1)
                for ub in range(USER_BLOCKS)
            ],
            axis=0,
        )

    recency_sums = weights[USER_BLOCKS * cells]

    def count_of(k):
        return jnp.concatenate(
            [
                jnp.concatenate(
                    [
                        jnp.broadcast_to(recency_sums[:, t : t + 1], (SUB, LANES))
                        for t in range(ub * cells + k * item_blocks, ub * cells + (k + 1) * item_blocks)
                    ],
                    axis=1,
                )
                for ub in range(USER_BLOCKS)
            ],
            axis=0,
        )

    def stacked(value):
        high, low = split_parts(value)
        return jnp.concatenate([high, low], axis=0).astype(jnp.bfloat16)

    def folded(pair):
        return (pair[:users, :features] + pair[:users, features:]) + (pair[users:, :features] + pair[users:, features:])

    def back(value, k):
        return jnp.dot(stacked(value), tall[k], preferred_element_type=jnp.float32)

    right = folded(sum(back(conf_of(k) + count_of(k), k) for k in range(STEPS)))

    def apply(direction):
        high, low = split_parts(direction)
        left = jnp.concatenate(
            [jnp.concatenate([high, high], axis=1), jnp.concatenate([low, low], axis=1)], axis=0
        ).astype(jnp.bfloat16)
        total = jnp.dot(left[:, :features], base_pair, preferred_element_type=jnp.float32)
        for k in range(STEPS):
            scores = jnp.dot(left, wide[k], preferred_element_type=jnp.float32)
            total = total + back((scores[:users] + scores[users:]) * conf_of(k), k)
        return folded(total)

    answer = jnp.zeros_like(right)
    residual = right
    direction = right
    norm_now = jnp.sum(residual * residual, axis=1, keepdims=True)
    for iteration in range(CG_ITERS):
        image = apply(direction)
        step = norm_now / jnp.sum(direction * image, axis=1, keepdims=True)
        answer = answer + step * direction
        if iteration + 1 < CG_ITERS:
            residual = residual - step * image
            norm_next = jnp.sum(residual * residual, axis=1, keepdims=True)
            direction = residual + (norm_next / norm_now) * direction
            norm_now = norm_next
    out[...] = answer


def body(item_emb, confidences, user_block, item_block, block_age, block_count):
    n_item, n_split = lax.axis_size("item"), lax.axis_size("split")
    rows, features = item_emb.shape
    block_users, block_items = confidences.shape[4:]
    item_blocks = rows // block_items
    half = pl.cdiv(USER_BLOCKS * STEPS * item_blocks + 1, 2)
    f32 = jnp.float32
    hbm = pl.BlockSpec(memory_space=pltpu.HBM)
    vmem = pl.BlockSpec(memory_space=pltpu.VMEM)
    params = pltpu.CompilerParams(vmem_limit_bytes=VMEM_LIMIT)
    half_tiles = jax.ShapeDtypeStruct((half, SUB, LANES), f32)

    def pair(value, axis):
        return lax.ppermute(value, axis, [(i, i ^ 1) for i in range(lax.axis_size(axis))])

    def shifted(value, axis, steps):
        count = lax.axis_size(axis)
        return lax.ppermute(value, axis, [(i, (i + steps) % count) for i in range(count)])

    slot_arrays = (user_block, item_block, block_age, block_count)
    keep, send = pl.pallas_call(
        functools.partial(weights_kernel, item_blocks, half),
        out_shape=[half_tiles, half_tiles],
        in_specs=[hbm] * 5,
        out_specs=[vmem] * 2,
        scratch_shapes=[pltpu.SMEM(a.shape, a.dtype) for a in slot_arrays]
        + [
            pltpu.VMEM(confidences.shape, confidences.dtype),
            pltpu.VMEM((2 * half, SUB, LANES), f32),
            pltpu.SemaphoreType.DMA((5,)),
        ],
        compiler_params=params,
        name="weights",
    )(*[pltpu.with_memory_space_constraint(a, pltpu.HBM) for a in (*slot_arrays, confidences)])
    keep = keep + pair(send, "split")

    second = shifted(item_emb, "item", 2)
    keep, sent = lax.optimization_barrier((keep, item_emb))
    first = lax.ppermute(sent, "item", [(i, (i + (3 if i % 2 else 1)) % n_item) for i in range(n_item)])
    total = keep
    for steps in range(2, n_split, 2):
        total = total + shifted(keep, "split", steps)
    ready, _ = lax.optimization_barrier((second, keep))
    two_gram = pl.pallas_call(
        gram_kernel,
        out_shape=jax.ShapeDtypeStruct((features, features), f32),
        in_specs=[vmem] * 2,
        out_specs=vmem,
        compiler_params=params,
        name="gram",
    )(item_emb, ready)
    four_gram = two_gram + pair(two_gram, "item")
    total, four_gram, ready = lax.optimization_barrier((total, four_gram, ready))
    third = pair(ready, "item")
    gram = four_gram
    for steps in range(STEPS, n_item, STEPS):
        gram = gram + shifted(four_gram, "item", steps)
    other = pair(total, "split")

    return pl.pallas_call(
        functools.partial(solve_kernel, item_blocks, half),
        out_shape=jax.ShapeDtypeStruct((USER_BLOCKS * block_users, features), f32),
        in_specs=[vmem] * (STEPS + 3),
        out_specs=vmem,
        scratch_shapes=[
            pltpu.VMEM((2 * half, SUB, LANES), f32),
            pltpu.VMEM((STEPS, 2 * features, rows), jnp.bfloat16),
            pltpu.VMEM((STEPS, rows, 2 * features), jnp.bfloat16),
        ],
        compiler_params=params,
        name="solve",
    )(item_emb, first, second, third, gram, total, other)


def solution(mesh):
    placed = (
        P("item", None),
        P("item", "split", None, None, None, None),
        P("item", "split", None, None),
        P("item", "split", None, None),
        P("item", "split", None, None),
        P("item", "split", None),
    )
    return jax.shard_map(
        body, mesh=mesh, in_specs=placed, out_specs=P("item", None), check_vma=False
    )
```

```python
import functools

import jax
import jax.numpy as jnp
from jax import lax
from jax.experimental import pallas as pl
from jax.experimental.pallas import tpu as pltpu
from jax.sharding import PartitionSpec as P

USER_BLOCKS = 3
STEPS = 4
CG_ITERS = 3
RIDGE = 0.1
SUM_COST = 400000000
BASE_COST = 1800000000
GRAM_COST = 0
VMEM_LIMIT = 16 * 2**20

SUB = 8
LANES = 128


def split_parts(value):
    high = value.astype(jnp.bfloat16).astype(jnp.float32)
    return high, value - high


def weights_kernel(item_blocks, half, *refs):
    arrays, (keep, send), held, (acc, arrived) = refs[:5], refs[5:7], refs[7:12], refs[12:]
    copies = [pltpu.make_async_copy(a, h, arrived.at[i]) for i, (a, h) in enumerate(zip(arrays, held))]
    for copy in copies:
        copy.start()
    acc[...] = jnp.zeros_like(acc)
    for copy in copies:
        copy.wait()
    users, items, ages, counts, conf = held
    cells = STEPS * item_blocks
    slots = conf.shape[3]
    upper = lax.rem(lax.axis_index("split"), 2)
    odd = lax.rem(lax.axis_index("item"), 2)
    lane = lax.broadcasted_iota(jnp.int32, (SUB, LANES), 1)
    recency_sums = jnp.zeros((SUB, LANES), jnp.float32)
    for k in range(STEPS):
        place = jnp.where(odd == 1, k, (STEPS - k) % STEPS)
        for j in range(slots):
            tile = users[0, 0, k, j] * cells + place * item_blocks + items[0, 0, k, j]
            age = jnp.full((SUB, LANES), ages[0, 0, k, j], jnp.int32).astype(jnp.float32)
            live = (j < counts[0, 0, k]).astype(jnp.float32)
            recency = 2.0 / (2.0 + age) * live
            acc[tile] = acc[tile] + conf[0, 0, k, j].astype(jnp.float32) * recency
            recency_sums = recency_sums + jnp.where(lane == tile, recency, 0.0)
    acc[USER_BLOCKS * cells] = recency_sums
    keep[...] = acc[pl.ds(upper * half, half)]
    send[...] = acc[pl.ds((1 - upper) * half, half)]


def gram_kernel(emb, second, out):
    total = 0.0
    for shard in (emb, second):
        high, low = split_parts(shard[...])
        upright = jnp.concatenate([high, low], axis=1).astype(jnp.bfloat16)
        across = jnp.concatenate([high.T, low.T], axis=0).astype(jnp.bfloat16)
        total = total + jnp.dot(across, upright, preferred_element_type=jnp.float32)
    total = total[:LANES] + total[LANES:]
    out[...] = total[:, :LANES] + total[:, LANES:]


def sum_kernel(*refs):
    refs[-1][...] = functools.reduce(jnp.add, [ref[...] for ref in refs[:-1]])


def base_kernel(gram, out):
    rows = lax.broadcasted_iota(jnp.int32, gram.shape, 0)
    columns = lax.broadcasted_iota(jnp.int32, gram.shape, 1)
    high, low = split_parts(gram[...] + jnp.where(rows == columns, RIDGE, 0.0))
    out[...] = jnp.concatenate([high, low], axis=1).astype(jnp.bfloat16)


def solve_kernel(item_blocks, half, *refs):
    shards = refs[:STEPS]
    base_pair, keep, other, out, weights, wide, tall = refs[STEPS:]
    cells = STEPS * item_blocks
    upper = lax.rem(lax.axis_index("split"), 2)
    users = USER_BLOCKS * SUB
    features = LANES

    weights[pl.ds(upper * half, half)] = keep[...]
    weights[pl.ds((1 - upper) * half, half)] = other[...]

    for k in range(STEPS):
        high, low = split_parts(shards[k][...])
        tall[k] = jnp.concatenate([high, low], axis=1).astype(jnp.bfloat16)
        wide[k] = jnp.concatenate([high.T, low.T], axis=0).astype(jnp.bfloat16)

    def conf_of(k):
        return jnp.concatenate(
            [
                jnp.concatenate([weights[ub * cells + k * item_blocks + i] for i in range(item_blocks)], axis=1)
                for ub in range(USER_BLOCKS)
            ],
            axis=0,
        )

    recency_sums = weights[USER_BLOCKS * cells]

    def count_of(k):
        return jnp.concatenate(
            [
                jnp.concatenate(
                    [
                        jnp.broadcast_to(recency_sums[:, t : t + 1], (SUB, LANES))
                        for t in range(ub * cells + k * item_blocks, ub * cells + (k + 1) * item_blocks)
                    ],
                    axis=1,
                )
                for ub in range(USER_BLOCKS)
            ],
            axis=0,
        )

    def stacked(value):
        high, low = split_parts(value)
        return jnp.concatenate([high, low], axis=0).astype(jnp.bfloat16)

    def folded(pair):
        return (pair[:users, :features] + pair[:users, features:]) + (pair[users:, :features] + pair[users:, features:])

    def back(value, k):
        return jnp.dot(stacked(value), tall[k], preferred_element_type=jnp.float32)

    right = folded(sum(back(conf_of(k) + count_of(k), k) for k in range(STEPS)))

    def scores_of(value):
        high, low = split_parts(value)
        left = jnp.concatenate(
            [jnp.concatenate([high, high], axis=1), jnp.concatenate([low, low], axis=1)], axis=0
        ).astype(jnp.bfloat16)
        through = folded(jnp.dot(left[:, :features], base_pair[...], preferred_element_type=jnp.float32))
        scores = []
        for k in range(STEPS):
            both = jnp.dot(left, wide[k], preferred_element_type=jnp.float32)
            scores.append(both[:users] + both[users:])
        return [through] + scores

    def curvature(direction, products, weighted):
        curve = direction * products[0]
        for k in range(STEPS):
            terms = weighted[k] * products[1 + k]
            for i in range(item_blocks):
                curve = curve + terms[:, i * LANES : (i + 1) * LANES]
        return jnp.sum(curve, axis=1, keepdims=True)

    confs = [conf_of(k) for k in range(STEPS)]
    answer = jnp.zeros_like(right)
    residual = right
    direction = right
    norm_now = jnp.sum(residual * residual, axis=1, keepdims=True)
    residual_products = scores_of(residual)
    products = residual_products
    for iteration in range(CG_ITERS):
        weighted = [products[1 + k] * confs[k] for k in range(STEPS)]
        step = norm_now / curvature(direction, products, weighted)
        answer = answer + step * direction
        if iteration + 1 < CG_ITERS:
            image = products[0] + folded(sum(back(weighted[k], k) for k in range(STEPS)))
            image_products = scores_of(image)
            residual = residual - step * image
            norm_next = jnp.sum(residual * residual, axis=1, keepdims=True)
            ratio = norm_next / norm_now
            direction = residual + ratio * direction
            residual_products = [r - step * i for r, i in zip(residual_products, image_products)]
            products = [r + ratio * p for r, p in zip(residual_products, products)]
            norm_now = norm_next
    out[...] = answer


def body(item_emb, confidences, user_block, item_block, block_age, block_count):
    n_item, n_split = lax.axis_size("item"), lax.axis_size("split")
    rows, features = item_emb.shape
    block_users, block_items = confidences.shape[4:]
    item_blocks = rows // block_items
    half = pl.cdiv(USER_BLOCKS * STEPS * item_blocks + 1, 2)
    f32 = jnp.float32
    hbm = pl.BlockSpec(memory_space=pltpu.HBM)
    vmem = pl.BlockSpec(memory_space=pltpu.VMEM)
    params = pltpu.CompilerParams(vmem_limit_bytes=VMEM_LIMIT)
    half_tiles = jax.ShapeDtypeStruct((half, SUB, LANES), f32)

    def pair(value, axis):
        return lax.ppermute(value, axis, [(i, i ^ 1) for i in range(lax.axis_size(axis))])

    def shifted(value, axis, steps):
        count = lax.axis_size(axis)
        return lax.ppermute(value, axis, [(i, (i + steps) % count) for i in range(count)])

    def cost(flops):
        return pl.CostEstimate(flops=flops, bytes_accessed=0, transcendentals=0)

    slot_arrays = (user_block, item_block, block_age, block_count)
    keep, send = pl.pallas_call(
        functools.partial(weights_kernel, item_blocks, half),
        out_shape=[half_tiles, half_tiles],
        in_specs=[hbm] * 5,
        out_specs=[vmem] * 2,
        scratch_shapes=[pltpu.SMEM(a.shape, a.dtype) for a in slot_arrays]
        + [
            pltpu.VMEM(confidences.shape, confidences.dtype),
            pltpu.VMEM((2 * half, SUB, LANES), f32),
            pltpu.SemaphoreType.DMA((5,)),
        ],
        compiler_params=params,
        name="weights",
    )(*[pltpu.with_memory_space_constraint(a, pltpu.HBM) for a in (*slot_arrays, confidences)])
    sent = item_emb
    with jax.named_scope("near_halves"):
        keep = keep + pair(send, "split")

    with jax.named_scope("second_shard"):
        second = shifted(sent, "item", 2)
    sent = item_emb
    with jax.named_scope("first_shard"):
        first = lax.ppermute(sent, "item", [(i, (i + (3 if i % 2 else 1)) % n_item) for i in range(n_item)])
    total = keep
    with jax.named_scope("far_halves"):
        for steps in range(2, n_split, 2):
            total = total + shifted(keep, "split", steps)
    ready, _ = lax.optimization_barrier((second, keep))
    two_gram = pl.pallas_call(
        gram_kernel,
        out_shape=jax.ShapeDtypeStruct((features, features), f32),
        in_specs=[vmem] * 2,
        out_specs=vmem,
        compiler_params=params,
        cost_estimate=cost(GRAM_COST),
        name="gram",
    )(item_emb, ready)
    with jax.named_scope("chip_gram"):
        four_gram = two_gram + pair(two_gram, "item")
    with jax.named_scope("all_gram"):
        grams = [shifted(four_gram, "item", steps) for steps in range(STEPS, n_item, STEPS)]
    gram = pl.pallas_call(
        sum_kernel,
        out_shape=jax.ShapeDtypeStruct((features, features), f32),
        in_specs=[vmem] * (1 + len(grams)),
        out_specs=vmem,
        compiler_params=params,
        cost_estimate=cost(SUM_COST),
        name="sum",
    )(four_gram, *grams)
    total, ready = lax.optimization_barrier((total, ready))
    with jax.named_scope("third_shard"):
        third = pair(ready, "item")
    gram, first = lax.optimization_barrier((gram, first))
    base_pair = pl.pallas_call(
        base_kernel,
        out_shape=jax.ShapeDtypeStruct((features, 2 * features), jnp.bfloat16),
        in_specs=[vmem],
        out_specs=vmem,
        compiler_params=params,
        cost_estimate=cost(BASE_COST),
        name="base",
    )(gram)
    with jax.named_scope("other_half"):
        other = pair(total, "split")

    return pl.pallas_call(
        functools.partial(solve_kernel, item_blocks, half),
        out_shape=jax.ShapeDtypeStruct((USER_BLOCKS * block_users, features), f32),
        in_specs=[vmem] * (STEPS + 3),
        out_specs=vmem,
        scratch_shapes=[
            pltpu.VMEM((2 * half, SUB, LANES), f32),
            pltpu.VMEM((STEPS, 2 * features, rows), jnp.bfloat16),
            pltpu.VMEM((STEPS, rows, 2 * features), jnp.bfloat16),
        ],
        compiler_params=params,
        name="solve",
    )(item_emb, first, second, third, base_pair, total, other)


def solution(mesh):
    placed = (
        P("item", None),
        P("item", "split", None, None, None, None),
        P("item", "split", None, None),
        P("item", "split", None, None),
        P("item", "split", None, None),
        P("item", "split", None),
    )
    return jax.shard_map(
        body, mesh=mesh, in_specs=placed, out_specs=P("item", None), check_vma=False
    )
```

```python
import functools

import jax
import jax.numpy as jnp
from jax import lax
from jax.experimental import pallas as pl
from jax.experimental.pallas import tpu as pltpu
from jax.sharding import PartitionSpec as P

USER_BLOCKS = 3
STEPS = 4
CG_ITERS = 3
RIDGE = 0.1
VMEM_LIMIT = 16 * 2**20

SUM_COST = 400_000_000
BASE_COST = 1_800_000_000

SUB = 8
LANES = 128


def split_parts(value):
    high = value.astype(jnp.bfloat16).astype(jnp.float32)
    return high, value - high


def weights_kernel(item_blocks, half, *refs):
    arrays, (keep, send), held, (acc, arrived) = refs[:5], refs[5:7], refs[7:12], refs[12:]
    copies = [pltpu.make_async_copy(a, h, arrived.at[i]) for i, (a, h) in enumerate(zip(arrays, held))]
    for copy in copies:
        copy.start()
    acc[...] = jnp.zeros_like(acc)
    for copy in copies:
        copy.wait()
    users, items, ages, counts, conf = held
    cells = STEPS * item_blocks
    slots = conf.shape[3]
    upper = lax.rem(lax.axis_index("split"), 2)
    odd = lax.rem(lax.axis_index("item"), 2)
    lane = lax.broadcasted_iota(jnp.int32, (SUB, LANES), 1)
    recency_sums = jnp.zeros((SUB, LANES), jnp.float32)
    for k in range(STEPS):
        place = jnp.where(odd == 1, k, (STEPS - k) % STEPS)
        for j in range(slots):
            tile = users[0, 0, k, j] * cells + place * item_blocks + items[0, 0, k, j]
            age = jnp.full((SUB, LANES), ages[0, 0, k, j], jnp.int32).astype(jnp.float32)
            live = (j < counts[0, 0, k]).astype(jnp.float32)
            recency = 2.0 / (2.0 + age) * live
            acc[tile] = acc[tile] + conf[0, 0, k, j].astype(jnp.float32) * recency
            recency_sums = recency_sums + jnp.where(lane == tile, recency, 0.0)
    acc[USER_BLOCKS * cells] = recency_sums
    keep[...] = acc[pl.ds(upper * half, half)]
    send[...] = acc[pl.ds((1 - upper) * half, half)]


def gram_kernel(emb, second, out):
    total = 0.0
    for shard in (emb, second):
        high, low = split_parts(shard[...])
        upright = jnp.concatenate([high, low], axis=1).astype(jnp.bfloat16)
        across = jnp.concatenate([high.T, low.T], axis=0).astype(jnp.bfloat16)
        total = total + jnp.dot(across, upright, preferred_element_type=jnp.float32)
    total = total[:LANES] + total[LANES:]
    out[...] = total[:, :LANES] + total[:, LANES:]


def sum_kernel(*refs):
    refs[-1][...] = functools.reduce(jnp.add, [ref[...] for ref in refs[:-1]])


def base_kernel(gram, out):
    rows = lax.broadcasted_iota(jnp.int32, gram.shape, 0)
    columns = lax.broadcasted_iota(jnp.int32, gram.shape, 1)
    high, low = split_parts(gram[...] + jnp.where(rows == columns, RIDGE, 0.0))
    out[...] = jnp.concatenate([high, low], axis=1).astype(jnp.bfloat16)


def solve_kernel(item_blocks, half, *refs):
    shards = refs[:STEPS]
    base_pair, keep, other, out, weights, wide, tall = refs[STEPS:]
    cells = STEPS * item_blocks
    upper = lax.rem(lax.axis_index("split"), 2)
    users = USER_BLOCKS * SUB
    features = LANES

    weights[pl.ds(upper * half, half)] = keep[...]
    weights[pl.ds((1 - upper) * half, half)] = other[...]

    for k in range(STEPS):
        high, low = split_parts(shards[k][...])
        tall[k] = jnp.concatenate([high, low], axis=1).astype(jnp.bfloat16)
        wide[k] = jnp.concatenate([high.T, low.T], axis=0).astype(jnp.bfloat16)

    def conf_of(k):
        return jnp.concatenate(
            [
                jnp.concatenate([weights[ub * cells + k * item_blocks + i] for i in range(item_blocks)], axis=1)
                for ub in range(USER_BLOCKS)
            ],
            axis=0,
        )

    recency_sums = weights[USER_BLOCKS * cells]

    def count_of(k):
        return jnp.concatenate(
            [
                jnp.concatenate(
                    [
                        jnp.broadcast_to(recency_sums[:, t : t + 1], (SUB, LANES))
                        for t in range(ub * cells + k * item_blocks, ub * cells + (k + 1) * item_blocks)
                    ],
                    axis=1,
                )
                for ub in range(USER_BLOCKS)
            ],
            axis=0,
        )

    def stacked(value):
        high, low = split_parts(value)
        return jnp.concatenate([high, low], axis=0).astype(jnp.bfloat16)

    def folded(pair):
        return (pair[:users, :features] + pair[:users, features:]) + (pair[users:, :features] + pair[users:, features:])

    def back(value, k):
        return jnp.dot(stacked(value), tall[k], preferred_element_type=jnp.float32)

    right = folded(sum(back(conf_of(k) + count_of(k), k) for k in range(STEPS)))

    def scores_of(direction):
        high, low = split_parts(direction)
        left = jnp.concatenate(
            [jnp.concatenate([high, high], axis=1), jnp.concatenate([low, low], axis=1)], axis=0
        ).astype(jnp.bfloat16)
        through = jnp.dot(left[:, :features], base_pair[...], preferred_element_type=jnp.float32)
        scores = []
        for k in range(STEPS):
            both = jnp.dot(left, wide[k], preferred_element_type=jnp.float32)
            scores.append(both[:users] + both[users:])
        return folded(through), scores

    confs = [conf_of(k) for k in range(STEPS)]
    answer = jnp.zeros_like(right)
    residual = right
    direction = right
    norm_now = jnp.sum(residual * residual, axis=1, keepdims=True)
    for iteration in range(CG_ITERS):
        through, scores = scores_of(direction)
        weighted = [scores[k] * confs[k] for k in range(STEPS)]
        curve = direction * through
        for k in range(STEPS):
            terms = weighted[k] * scores[k]
            for i in range(item_blocks):
                curve = curve + terms[:, i * LANES : (i + 1) * LANES]
        step = norm_now / jnp.sum(curve, axis=1, keepdims=True)
        answer = answer + step * direction
        if iteration + 1 < CG_ITERS:
            image = through + folded(sum(back(weighted[k], k) for k in range(STEPS)))
            residual = residual - step * image
            norm_next = jnp.sum(residual * residual, axis=1, keepdims=True)
            direction = residual + (norm_next / norm_now) * direction
            norm_now = norm_next
    out[...] = answer


def body(item_emb, confidences, user_block, item_block, block_age, block_count):
    n_item, n_split = lax.axis_size("item"), lax.axis_size("split")
    rows, features = item_emb.shape
    block_users, block_items = confidences.shape[4:]
    item_blocks = rows // block_items
    half = pl.cdiv(USER_BLOCKS * STEPS * item_blocks + 1, 2)
    f32 = jnp.float32
    hbm = pl.BlockSpec(memory_space=pltpu.HBM)
    vmem = pl.BlockSpec(memory_space=pltpu.VMEM)
    params = pltpu.CompilerParams(vmem_limit_bytes=VMEM_LIMIT)
    half_tiles = jax.ShapeDtypeStruct((half, SUB, LANES), f32)

    def pair(value, axis):
        return lax.ppermute(value, axis, [(i, i ^ 1) for i in range(lax.axis_size(axis))])

    def shifted(value, axis, steps):
        count = lax.axis_size(axis)
        return lax.ppermute(value, axis, [(i, (i + steps) % count) for i in range(count)])

    def cost(flops):
        return pl.CostEstimate(flops=flops, bytes_accessed=0, transcendentals=0)

    slot_arrays = (user_block, item_block, block_age, block_count)
    keep, send = pl.pallas_call(
        functools.partial(weights_kernel, item_blocks, half),
        out_shape=[half_tiles, half_tiles],
        in_specs=[hbm] * 5,
        out_specs=[vmem] * 2,
        scratch_shapes=[pltpu.SMEM(a.shape, a.dtype) for a in slot_arrays]
        + [
            pltpu.VMEM(confidences.shape, confidences.dtype),
            pltpu.VMEM((2 * half, SUB, LANES), f32),
            pltpu.SemaphoreType.DMA((5,)),
        ],
        compiler_params=params,
        name="weights",
    )(*[pltpu.with_memory_space_constraint(a, pltpu.HBM) for a in (*slot_arrays, confidences)])
    with jax.named_scope("near_halves"):
        keep = keep + pair(send, "split")

    with jax.named_scope("second_shard"):
        second = shifted(item_emb, "item", 2)
    with jax.named_scope("first_shard"):
        first = lax.ppermute(item_emb, "item", [(i, (i + (3 if i % 2 else 1)) % n_item) for i in range(n_item)])
    total = keep
    with jax.named_scope("far_halves"):
        for steps in range(2, n_split, 2):
            total = total + shifted(keep, "split", steps)
    ready, _ = lax.optimization_barrier((second, keep))
    two_gram = pl.pallas_call(
        gram_kernel,
        out_shape=jax.ShapeDtypeStruct((features, features), f32),
        in_specs=[vmem] * 2,
        out_specs=vmem,
        compiler_params=params,
        name="gram",
    )(item_emb, ready)
    with jax.named_scope("chip_gram"):
        four_gram = two_gram + pair(two_gram, "item")
    with jax.named_scope("all_gram"):
        grams = [shifted(four_gram, "item", steps) for steps in range(STEPS, n_item, STEPS)]
    gram = pl.pallas_call(
        sum_kernel,
        out_shape=jax.ShapeDtypeStruct((features, features), f32),
        in_specs=[vmem] * (1 + len(grams)),
        out_specs=vmem,
        compiler_params=params,
        cost_estimate=cost(SUM_COST),
        name="sum",
    )(four_gram, *grams)
    total, ready = lax.optimization_barrier((total, ready))
    with jax.named_scope("third_shard"):
        third = pair(ready, "item")
    gram, first = lax.optimization_barrier((gram, first))
    base_pair = pl.pallas_call(
        base_kernel,
        out_shape=jax.ShapeDtypeStruct((features, 2 * features), jnp.bfloat16),
        in_specs=[vmem],
        out_specs=vmem,
        compiler_params=params,
        cost_estimate=cost(BASE_COST),
        name="base",
    )(gram)
    with jax.named_scope("other_half"):
        other = pair(total, "split")

    return pl.pallas_call(
        functools.partial(solve_kernel, item_blocks, half),
        out_shape=jax.ShapeDtypeStruct((USER_BLOCKS * block_users, features), f32),
        in_specs=[vmem] * (STEPS + 3),
        out_specs=vmem,
        scratch_shapes=[
            pltpu.VMEM((2 * half, SUB, LANES), f32),
            pltpu.VMEM((STEPS, 2 * features, rows), jnp.bfloat16),
            pltpu.VMEM((STEPS, rows, 2 * features), jnp.bfloat16),
        ],
        compiler_params=params,
        name="solve",
    )(item_emb, first, second, third, base_pair, total, other)


def solution(mesh):
    placed = (
        P("item", None),
        P("item", "split", None, None, None, None),
        P("item", "split", None, None),
        P("item", "split", None, None),
        P("item", "split", None, None),
        P("item", "split", None),
    )
    return jax.shard_map(
        body, mesh=mesh, in_specs=placed, out_specs=P("item", None), check_vma=False
    )
```

```python
import functools

import jax
import jax.numpy as jnp
from jax import lax
from jax.experimental import pallas as pl
from jax.experimental.pallas import tpu as pltpu
from jax.sharding import PartitionSpec as P

USER_BLOCKS = 3
STEPS = 4
CG_ITERS = 3
RIDGE = 0.1
VMEM_LIMIT = 16 * 2**20

SUM_COST = 600000000
BASE_COST = 1900000000

SUB = 8
LANES = 128


def split_parts(value):
    high = value.astype(jnp.bfloat16).astype(jnp.float32)
    return high, value - high


def weights_kernel(item_blocks, half, *refs):
    arrays, (keep, send), held, (acc, arrived) = refs[:5], refs[5:7], refs[7:12], refs[12:]
    copies = [pltpu.make_async_copy(a, h, arrived.at[i]) for i, (a, h) in enumerate(zip(arrays, held))]
    for copy in copies:
        copy.start()
    acc[...] = jnp.zeros_like(acc)
    for copy in copies:
        copy.wait()
    users, items, ages, counts, conf = held
    cells = STEPS * item_blocks
    slots = conf.shape[3]
    upper = lax.rem(lax.axis_index("split"), 2)
    odd = lax.rem(lax.axis_index("item"), 2)
    lane = lax.broadcasted_iota(jnp.int32, (SUB, LANES), 1)
    recency_sums = jnp.zeros((SUB, LANES), jnp.float32)
    for k in range(STEPS):
        place = jnp.where(odd == 1, k, (STEPS - k) % STEPS)
        for j in range(slots):
            tile = users[0, 0, k, j] * cells + place * item_blocks + items[0, 0, k, j]
            age = jnp.full((SUB, LANES), ages[0, 0, k, j], jnp.int32).astype(jnp.float32)
            live = (j < counts[0, 0, k]).astype(jnp.float32)
            recency = 2.0 / (2.0 + age) * live
            acc[tile] = acc[tile] + conf[0, 0, k, j].astype(jnp.float32) * recency
            recency_sums = recency_sums + jnp.where(lane == tile, recency, 0.0)
    acc[USER_BLOCKS * cells] = recency_sums
    keep[...] = acc[pl.ds(upper * half, half)]
    send[...] = acc[pl.ds((1 - upper) * half, half)]


def gram_kernel(emb, second, out):
    total = 0.0
    for shard in (emb, second):
        high, low = split_parts(shard[...])
        upright = jnp.concatenate([high, low], axis=1).astype(jnp.bfloat16)
        across = jnp.concatenate([high.T, low.T], axis=0).astype(jnp.bfloat16)
        total = total + jnp.dot(across, upright, preferred_element_type=jnp.float32)
    total = total[:LANES] + total[LANES:]
    out[...] = total[:, :LANES] + total[:, LANES:]


def sum_kernel(*refs):
    refs[-1][...] = functools.reduce(jnp.add, [ref[...] for ref in refs[:-1]])


def place_kernel(mine, other, low, high):
    upper = lax.rem(lax.axis_index("split"), 2)
    low[...] = jnp.where(upper == 1, other[...], mine[...])
    high[...] = jnp.where(upper == 1, mine[...], other[...])


def base_kernel(gram, out):
    rows = lax.broadcasted_iota(jnp.int32, gram.shape, 0)
    columns = lax.broadcasted_iota(jnp.int32, gram.shape, 1)
    high, low = split_parts(gram[...] + jnp.where(rows == columns, RIDGE, 0.0))
    out[...] = jnp.concatenate([high, low], axis=1).astype(jnp.bfloat16)


def solve_kernel(item_blocks, half, *refs):
    shards = refs[:STEPS]
    base_pair, low, high, out, weights, wide, tall = refs[STEPS:]
    cells = STEPS * item_blocks
    users = USER_BLOCKS * SUB
    features = LANES

    weights[0:half] = low[...]
    weights[half:] = high[...]

    for k in range(STEPS):
        high, low = split_parts(shards[k][...])
        tall[k] = jnp.concatenate([high, low], axis=1).astype(jnp.bfloat16)
        wide[k] = jnp.concatenate([high.T, low.T], axis=0).astype(jnp.bfloat16)

    def conf_of(k):
        return jnp.concatenate(
            [
                jnp.concatenate([weights[ub * cells + k * item_blocks + i] for i in range(item_blocks)], axis=1)
                for ub in range(USER_BLOCKS)
            ],
            axis=0,
        )

    recency_sums = weights[USER_BLOCKS * cells]

    def count_of(k):
        return jnp.concatenate(
            [
                jnp.concatenate(
                    [
                        jnp.broadcast_to(recency_sums[:, t : t + 1], (SUB, LANES))
                        for t in range(ub * cells + k * item_blocks, ub * cells + (k + 1) * item_blocks)
                    ],
                    axis=1,
                )
                for ub in range(USER_BLOCKS)
            ],
            axis=0,
        )

    def stacked(value):
        high, low = split_parts(value)
        return jnp.concatenate([high, low], axis=0).astype(jnp.bfloat16)

    def folded(pair):
        return (pair[:users, :features] + pair[:users, features:]) + (pair[users:, :features] + pair[users:, features:])

    def back(value, k):
        return jnp.dot(stacked(value), tall[k], preferred_element_type=jnp.float32)

    right = folded(sum(back(conf_of(k) + count_of(k), k) for k in range(STEPS)))

    def scores_of(direction):
        high, low = split_parts(direction)
        left = jnp.concatenate(
            [jnp.concatenate([high, high], axis=1), jnp.concatenate([low, low], axis=1)], axis=0
        ).astype(jnp.bfloat16)
        through = jnp.dot(left[:, :features], base_pair[...], preferred_element_type=jnp.float32)
        scores = []
        for k in range(STEPS):
            both = jnp.dot(left, wide[k], preferred_element_type=jnp.float32)
            scores.append(both[:users] + both[users:])
        return folded(through), scores

    confs = [conf_of(k) for k in range(STEPS)]
    answer = jnp.zeros_like(right)
    residual = right
    direction = right
    norm_now = jnp.sum(residual * residual, axis=1, keepdims=True)
    for iteration in range(CG_ITERS):
        through, scores = scores_of(direction)
        weighted = [scores[k] * confs[k] for k in range(STEPS)]
        curve = direction * through
        for k in range(STEPS):
            terms = weighted[k] * scores[k]
            for i in range(item_blocks):
                curve = curve + terms[:, i * LANES : (i + 1) * LANES]
        step = norm_now / jnp.sum(curve, axis=1, keepdims=True)
        answer = answer + step * direction
        if iteration + 1 < CG_ITERS:
            image = through + folded(sum(back(weighted[k], k) for k in range(STEPS)))
            residual = residual - step * image
            norm_next = jnp.sum(residual * residual, axis=1, keepdims=True)
            direction = residual + (norm_next / norm_now) * direction
            norm_now = norm_next
    out[...] = answer


def body(item_emb, confidences, user_block, item_block, block_age, block_count):
    n_item, n_split = lax.axis_size("item"), lax.axis_size("split")
    rows, features = item_emb.shape
    block_users, block_items = confidences.shape[4:]
    item_blocks = rows // block_items
    half = pl.cdiv(USER_BLOCKS * STEPS * item_blocks + 1, 2)
    f32 = jnp.float32
    hbm = pl.BlockSpec(memory_space=pltpu.HBM)
    vmem = pl.BlockSpec(memory_space=pltpu.VMEM)
    params = pltpu.CompilerParams(vmem_limit_bytes=VMEM_LIMIT)
    half_tiles = jax.ShapeDtypeStruct((half, SUB, LANES), f32)

    def pair(value, axis):
        return lax.ppermute(value, axis, [(i, i ^ 1) for i in range(lax.axis_size(axis))])

    def shifted(value, axis, steps):
        count = lax.axis_size(axis)
        return lax.ppermute(value, axis, [(i, (i + steps) % count) for i in range(count)])

    def cost(flops):
        return pl.CostEstimate(flops=flops, bytes_accessed=0, transcendentals=0)

    slot_arrays = (user_block, item_block, block_age, block_count)
    keep, send = pl.pallas_call(
        functools.partial(weights_kernel, item_blocks, half),
        out_shape=[half_tiles, half_tiles],
        in_specs=[hbm] * 5,
        out_specs=[vmem] * 2,
        scratch_shapes=[pltpu.SMEM(a.shape, a.dtype) for a in slot_arrays]
        + [
            pltpu.VMEM(confidences.shape, confidences.dtype),
            pltpu.VMEM((2 * half, SUB, LANES), f32),
            pltpu.SemaphoreType.DMA((5,)),
        ],
        compiler_params=params,
        name="weights",
    )(*[pltpu.with_memory_space_constraint(a, pltpu.HBM) for a in (*slot_arrays, confidences)])
    with jax.named_scope("near_halves"):
        keep = keep + pair(send, "split")

    with jax.named_scope("second_shard"):
        second = shifted(item_emb, "item", 2)
    with jax.named_scope("first_shard"):
        first = lax.ppermute(item_emb, "item", [(i, (i + (3 if i % 2 else 1)) % n_item) for i in range(n_item)])
    total = keep
    with jax.named_scope("far_halves"):
        for steps in range(2, n_split, 2):
            total = total + shifted(keep, "split", steps)
    ready, _ = lax.optimization_barrier((second, keep))
    two_gram = pl.pallas_call(
        gram_kernel,
        out_shape=jax.ShapeDtypeStruct((features, features), f32),
        in_specs=[vmem] * 2,
        out_specs=vmem,
        compiler_params=params,
        name="gram",
    )(item_emb, ready)
    with jax.named_scope("chip_gram"):
        four_gram = two_gram + pair(two_gram, "item")
    with jax.named_scope("all_gram"):
        grams = [shifted(four_gram, "item", steps) for steps in range(STEPS, n_item, STEPS)]
    gram = pl.pallas_call(
        sum_kernel,
        out_shape=jax.ShapeDtypeStruct((features, features), f32),
        in_specs=[vmem] * (1 + len(grams)),
        out_specs=vmem,
        compiler_params=params,
        cost_estimate=cost(SUM_COST),
        name="sum",
    )(four_gram, *grams)
    total, ready = lax.optimization_barrier((total, ready))
    with jax.named_scope("third_shard"):
        third = pair(ready, "item")
    gram, first = lax.optimization_barrier((gram, first))
    with jax.named_scope("other_half"):
        other = pair(total, "split")
    other, gram = lax.optimization_barrier((other, gram))
    low, high = pl.pallas_call(
        place_kernel,
        out_shape=[half_tiles] * 2,
        in_specs=[vmem] * 2,
        out_specs=[vmem] * 2,
        compiler_params=params,
        name="place",
    )(total, other)

    base_pair = pl.pallas_call(
        base_kernel,
        out_shape=jax.ShapeDtypeStruct((features, 2 * features), jnp.bfloat16),
        in_specs=[vmem],
        out_specs=vmem,
        compiler_params=params,
        cost_estimate=cost(BASE_COST),
        name="base",
    )(gram)
    return pl.pallas_call(
        functools.partial(solve_kernel, item_blocks, half),
        out_shape=jax.ShapeDtypeStruct((USER_BLOCKS * block_users, features), f32),
        in_specs=[vmem] * (STEPS + 3),
        out_specs=vmem,
        scratch_shapes=[
            pltpu.VMEM((2 * half, SUB, LANES), f32),
            pltpu.VMEM((STEPS, 2 * features, rows), jnp.bfloat16),
            pltpu.VMEM((STEPS, rows, 2 * features), jnp.bfloat16),
        ],
        compiler_params=params,
        name="solve",
    )(item_emb, first, second, third, base_pair, low, high)


def solution(mesh):
    placed = (
        P("item", None),
        P("item", "split", None, None, None, None),
        P("item", "split", None, None),
        P("item", "split", None, None),
        P("item", "split", None, None),
        P("item", "split", None),
    )
    return jax.shard_map(
        body, mesh=mesh, in_specs=placed, out_specs=P("item", None), check_vma=False
    )
```

```python
import functools

import jax
import jax.numpy as jnp
from jax import lax
from jax.experimental import pallas as pl
from jax.experimental.pallas import tpu as pltpu
from jax.sharding import PartitionSpec as P

USER_BLOCKS = 3
STEPS = 4
CG_ITERS = 3
RIDGE = 0.1
VMEM_LIMIT = 16 * 2**20

SUM_COST = 600000000
BASE_COST = 1900000000

SUB = 8
LANES = 128


def split_parts(value):
    high = value.astype(jnp.bfloat16).astype(jnp.float32)
    return high, value - high


def weights_kernel(item_blocks, half, *refs):
    arrays, (keep, send), held, (acc, arrived) = refs[:5], refs[5:7], refs[7:12], refs[12:]
    copies = [pltpu.make_async_copy(a, h, arrived.at[i]) for i, (a, h) in enumerate(zip(arrays, held))]
    for copy in copies:
        copy.start()
    acc[...] = jnp.zeros_like(acc)
    for copy in copies:
        copy.wait()
    users, items, ages, counts, conf = held
    cells = STEPS * item_blocks
    slots = conf.shape[3]
    upper = lax.rem(lax.axis_index("split"), 2)
    odd = lax.rem(lax.axis_index("item"), 2)
    lane = lax.broadcasted_iota(jnp.int32, (SUB, LANES), 1)
    recency_sums = jnp.zeros((SUB, LANES), jnp.float32)
    for k in range(STEPS):
        place = jnp.where(odd == 1, k, (STEPS - k) % STEPS)
        for j in range(slots):
            tile = users[0, 0, k, j] * cells + place * item_blocks + items[0, 0, k, j]
            age = jnp.full((SUB, LANES), ages[0, 0, k, j], jnp.int32).astype(jnp.float32)
            live = (j < counts[0, 0, k]).astype(jnp.float32)
            recency = 2.0 / (2.0 + age) * live
            acc[tile] = acc[tile] + conf[0, 0, k, j].astype(jnp.float32) * recency
            recency_sums = recency_sums + jnp.where(lane == tile, recency, 0.0)
    acc[USER_BLOCKS * cells] = recency_sums
    keep[...] = acc[pl.ds(upper * half, half)]
    send[...] = acc[pl.ds((1 - upper) * half, half)]


def gram_kernel(emb, second, out):
    total = 0.0
    for shard in (emb, second):
        high, low = split_parts(shard[...])
        upright = jnp.concatenate([high, low], axis=1).astype(jnp.bfloat16)
        across = jnp.concatenate([high.T, low.T], axis=0).astype(jnp.bfloat16)
        total = total + jnp.dot(across, upright, preferred_element_type=jnp.float32)
    total = total[:LANES] + total[LANES:]
    out[...] = total[:, :LANES] + total[:, LANES:]


def sum_kernel(*refs):
    refs[-1][...] = functools.reduce(jnp.add, [ref[...] for ref in refs[:-1]])


def place_kernel(mine, other, low, high):
    upper = lax.rem(lax.axis_index("split"), 2)
    low[...] = jnp.where(upper == 1, other[...], mine[...])
    high[...] = jnp.where(upper == 1, mine[...], other[...])


def base_kernel(gram, out):
    rows = lax.broadcasted_iota(jnp.int32, gram.shape, 0)
    columns = lax.broadcasted_iota(jnp.int32, gram.shape, 1)
    high, low = split_parts(gram[...] + jnp.where(rows == columns, RIDGE, 0.0))
    out[...] = jnp.concatenate([high, low], axis=1).astype(jnp.bfloat16)


def solve_kernel(item_blocks, half, *refs):
    shards = refs[:STEPS]
    base_pair, lower, upper, out, wide, tall = refs[STEPS:]
    cells = STEPS * item_blocks
    users = USER_BLOCKS * SUB
    features = LANES

    def tile(index):
        return lower[index] if index < half else upper[index - half]

    for k in range(STEPS):
        high, low = split_parts(shards[k][...])
        tall[k] = jnp.concatenate([high, low], axis=1).astype(jnp.bfloat16)
        wide[k] = jnp.concatenate([high.T, low.T], axis=0).astype(jnp.bfloat16)

    def conf_of(k):
        return jnp.concatenate(
            [
                jnp.concatenate([tile(ub * cells + k * item_blocks + i) for i in range(item_blocks)], axis=1)
                for ub in range(USER_BLOCKS)
            ],
            axis=0,
        )

    recency_sums = tile(USER_BLOCKS * cells)

    def count_of(k):
        return jnp.concatenate(
            [
                jnp.concatenate(
                    [
                        jnp.broadcast_to(recency_sums[:, t : t + 1], (SUB, LANES))
                        for t in range(ub * cells + k * item_blocks, ub * cells + (k + 1) * item_blocks)
                    ],
                    axis=1,
                )
                for ub in range(USER_BLOCKS)
            ],
            axis=0,
        )

    def stacked(value):
        high, low = split_parts(value)
        return jnp.concatenate([high, low], axis=0).astype(jnp.bfloat16)

    def folded(pair):
        return (pair[:users, :features] + pair[:users, features:]) + (pair[users:, :features] + pair[users:, features:])

    def back(value, k):
        return jnp.dot(stacked(value), tall[k], preferred_element_type=jnp.float32)

    right = folded(sum(back(conf_of(k) + count_of(k), k) for k in range(STEPS)))

    def scores_of(value):
        high, low = split_parts(value)
        left = jnp.concatenate(
            [jnp.concatenate([high, high], axis=1), jnp.concatenate([low, low], axis=1)], axis=0
        ).astype(jnp.bfloat16)
        through = jnp.dot(left[:, :features], base_pair[...], preferred_element_type=jnp.float32)
        scores = []
        for k in range(STEPS):
            both = jnp.dot(left, wide[k], preferred_element_type=jnp.float32)
            scores.append(both[:users] + both[users:])
        return folded(through), scores

    confs = [conf_of(k) for k in range(STEPS)]
    answer = jnp.zeros_like(right)
    residual = right
    direction = right
    norm_now = jnp.sum(residual * residual, axis=1, keepdims=True)
    through, scores = scores_of(right)
    for iteration in range(CG_ITERS):
        weighted = [scores[k] * confs[k] for k in range(STEPS)]
        curve = direction * through
        for k in range(STEPS):
            terms = weighted[k] * scores[k]
            for i in range(item_blocks):
                curve = curve + terms[:, i * LANES : (i + 1) * LANES]
        step = norm_now / jnp.sum(curve, axis=1, keepdims=True)
        answer = answer + step * direction
        if iteration + 1 < CG_ITERS:
            image = through + folded(sum(back(weighted[k], k) for k in range(STEPS)))
            residual = residual - step * image
            norm_next = jnp.sum(residual * residual, axis=1, keepdims=True)
            through_next, scores_next = scores_of(residual)
            ratio = norm_next / norm_now
            direction = residual + ratio * direction
            through = through_next + ratio * through
            scores = [n + ratio * s for n, s in zip(scores_next, scores)]
            norm_now = norm_next
    out[...] = answer


def body(item_emb, confidences, user_block, item_block, block_age, block_count):
    n_item, n_split = lax.axis_size("item"), lax.axis_size("split")
    rows, features = item_emb.shape
    block_users, block_items = confidences.shape[4:]
    item_blocks = rows // block_items
    half = pl.cdiv(USER_BLOCKS * STEPS * item_blocks + 1, 2)
    f32 = jnp.float32
    hbm = pl.BlockSpec(memory_space=pltpu.HBM)
    vmem = pl.BlockSpec(memory_space=pltpu.VMEM)
    params = pltpu.CompilerParams(vmem_limit_bytes=VMEM_LIMIT)
    half_tiles = jax.ShapeDtypeStruct((half, SUB, LANES), f32)

    def pair(value, axis):
        return lax.ppermute(value, axis, [(i, i ^ 1) for i in range(lax.axis_size(axis))])

    def shifted(value, axis, steps):
        count = lax.axis_size(axis)
        return lax.ppermute(value, axis, [(i, (i + steps) % count) for i in range(count)])

    def cost(flops):
        return pl.CostEstimate(flops=flops, bytes_accessed=0, transcendentals=0)

    slot_arrays = (user_block, item_block, block_age, block_count)
    keep, send = pl.pallas_call(
        functools.partial(weights_kernel, item_blocks, half),
        out_shape=[half_tiles, half_tiles],
        in_specs=[hbm] * 5,
        out_specs=[vmem] * 2,
        scratch_shapes=[pltpu.SMEM(a.shape, a.dtype) for a in slot_arrays]
        + [
            pltpu.VMEM(confidences.shape, confidences.dtype),
            pltpu.VMEM((2 * half, SUB, LANES), f32),
            pltpu.SemaphoreType.DMA((5,)),
        ],
        compiler_params=params,
        name="weights",
    )(*[pltpu.with_memory_space_constraint(a, pltpu.HBM) for a in (*slot_arrays, confidences)])
    with jax.named_scope("near_halves"):
        keep = keep + pair(send, "split")

    with jax.named_scope("second_shard"):
        second = shifted(item_emb, "item", 2)
    with jax.named_scope("first_shard"):
        first = lax.ppermute(item_emb, "item", [(i, (i + (3 if i % 2 else 1)) % n_item) for i in range(n_item)])
    total = keep
    with jax.named_scope("far_halves"):
        for steps in range(2, n_split, 2):
            total = total + shifted(keep, "split", steps)
    ready, _ = lax.optimization_barrier((second, keep))
    two_gram = pl.pallas_call(
        gram_kernel,
        out_shape=jax.ShapeDtypeStruct((features, features), f32),
        in_specs=[vmem] * 2,
        out_specs=vmem,
        compiler_params=params,
        name="gram",
    )(item_emb, ready)
    with jax.named_scope("chip_gram"):
        four_gram = two_gram + pair(two_gram, "item")
    with jax.named_scope("all_gram"):
        grams = [shifted(four_gram, "item", steps) for steps in range(STEPS, n_item, STEPS)]
    gram = pl.pallas_call(
        sum_kernel,
        out_shape=jax.ShapeDtypeStruct((features, features), f32),
        in_specs=[vmem] * (1 + len(grams)),
        out_specs=vmem,
        compiler_params=params,
        cost_estimate=cost(SUM_COST),
        name="sum",
    )(four_gram, *grams)
    total, ready = lax.optimization_barrier((total, ready))
    with jax.named_scope("third_shard"):
        third = pair(ready, "item")
    gram, first = lax.optimization_barrier((gram, first))
    with jax.named_scope("other_half"):
        other = pair(total, "split")
    other, gram = lax.optimization_barrier((other, gram))
    low, high = pl.pallas_call(
        place_kernel,
        out_shape=[half_tiles] * 2,
        in_specs=[vmem] * 2,
        out_specs=[vmem] * 2,
        compiler_params=params,
        name="place",
    )(total, other)

    base_pair = pl.pallas_call(
        base_kernel,
        out_shape=jax.ShapeDtypeStruct((features, 2 * features), jnp.bfloat16),
        in_specs=[vmem],
        out_specs=vmem,
        compiler_params=params,
        cost_estimate=cost(BASE_COST),
        name="base",
    )(gram)
    return pl.pallas_call(
        functools.partial(solve_kernel, item_blocks, half),
        out_shape=jax.ShapeDtypeStruct((USER_BLOCKS * block_users, features), f32),
        in_specs=[vmem] * (STEPS + 3),
        out_specs=vmem,
        scratch_shapes=[
            pltpu.VMEM((STEPS, 2 * features, rows), jnp.bfloat16),
            pltpu.VMEM((STEPS, rows, 2 * features), jnp.bfloat16),
        ],
        compiler_params=params,
        name="solve",
    )(item_emb, first, second, third, base_pair, low, high)


def solution(mesh):
    placed = (
        P("item", None),
        P("item", "split", None, None, None, None),
        P("item", "split", None, None),
        P("item", "split", None, None),
        P("item", "split", None, None),
        P("item", "split", None),
    )
    return jax.shard_map(
        body, mesh=mesh, in_specs=placed, out_specs=P("item", None), check_vma=False
    )
```

```python
import functools

import jax
import jax.numpy as jnp
from jax import lax
from jax.experimental import pallas as pl
from jax.experimental.pallas import tpu as pltpu
from jax.sharding import PartitionSpec as P

USER_BLOCKS = 3
STEPS = 4
CG_ITERS = 3
RIDGE = 0.1
VMEM_LIMIT = 16 * 2**20

SUM_COST = 600000000
BASE_COST = 1900000000

SUB = 8
LANES = 128


def split_parts(value):
    high = value.astype(jnp.bfloat16).astype(jnp.float32)
    return high, value - high


def weights_kernel(item_blocks, half, *refs):
    arrays, (keep, send), held, (acc, arrived) = refs[:5], refs[5:7], refs[7:12], refs[12:]
    copies = [pltpu.make_async_copy(a, h, arrived.at[i]) for i, (a, h) in enumerate(zip(arrays, held))]
    for copy in copies:
        copy.start()
    acc[...] = jnp.zeros_like(acc)
    for copy in copies:
        copy.wait()
    users, items, ages, counts, conf = held
    cells = STEPS * item_blocks
    slots = conf.shape[3]
    upper = lax.rem(lax.axis_index("split"), 2)
    odd = lax.rem(lax.axis_index("item"), 2)
    lane = lax.broadcasted_iota(jnp.int32, (SUB, LANES), 1)
    recency_sums = jnp.zeros((SUB, LANES), jnp.float32)
    for k in range(STEPS):
        place = jnp.where(odd == 1, k, (STEPS - k) % STEPS)
        for j in range(slots):
            tile = users[0, 0, k, j] * cells + place * item_blocks + items[0, 0, k, j]
            age = jnp.full((SUB, LANES), ages[0, 0, k, j], jnp.int32).astype(jnp.float32)
            live = (j < counts[0, 0, k]).astype(jnp.float32)
            recency = 2.0 / (2.0 + age) * live
            acc[tile] = acc[tile] + conf[0, 0, k, j].astype(jnp.float32) * recency
            recency_sums = recency_sums + jnp.where(lane == tile, recency, 0.0)
    acc[USER_BLOCKS * cells] = recency_sums
    keep[...] = acc[pl.ds(upper * half, half)]
    send[...] = acc[pl.ds((1 - upper) * half, half)]


def gram_kernel(emb, second, out):
    total = 0.0
    for shard in (emb, second):
        high, low = split_parts(shard[...])
        upright = jnp.concatenate([high, low], axis=1).astype(jnp.bfloat16)
        across = jnp.concatenate([high.T, low.T], axis=0).astype(jnp.bfloat16)
        total = total + jnp.dot(across, upright, preferred_element_type=jnp.float32)
    total = total[:LANES] + total[LANES:]
    out[...] = total[:, :LANES] + total[:, LANES:]


def sum_kernel(*refs):
    refs[-1][...] = functools.reduce(jnp.add, [ref[...] for ref in refs[:-1]])


def place_kernel(mine, other, low, high):
    upper = lax.rem(lax.axis_index("split"), 2)
    low[...] = jnp.where(upper == 1, other[...], mine[...])
    high[...] = jnp.where(upper == 1, mine[...], other[...])


def base_kernel(gram, out):
    rows = lax.broadcasted_iota(jnp.int32, gram.shape, 0)
    columns = lax.broadcasted_iota(jnp.int32, gram.shape, 1)
    high, low = split_parts(gram[...] + jnp.where(rows == columns, RIDGE, 0.0))
    out[...] = jnp.concatenate([high, low], axis=1).astype(jnp.bfloat16)


def solve_kernel(item_blocks, half, *refs):
    shards = refs[:STEPS]
    base_pair, lower, upper, out, wide, tall = refs[STEPS:]
    cells = STEPS * item_blocks
    users = USER_BLOCKS * SUB
    features = LANES
    rows = shards[0].shape[0]

    def tile(index):
        return lower[index] if index < half else upper[index - half]

    for k in range(STEPS):
        high, low = split_parts(shards[k][...])
        tall[k * rows : (k + 1) * rows] = jnp.concatenate([high, low], axis=1).astype(jnp.bfloat16)
        wide[k] = jnp.concatenate([high.T, low.T], axis=0).astype(jnp.bfloat16)

    def conf_of(k):
        return jnp.concatenate(
            [
                jnp.concatenate([tile(ub * cells + k * item_blocks + i) for i in range(item_blocks)], axis=1)
                for ub in range(USER_BLOCKS)
            ],
            axis=0,
        )

    recency_sums = tile(USER_BLOCKS * cells)

    def count_of(k):
        return jnp.concatenate(
            [
                jnp.concatenate(
                    [
                        jnp.broadcast_to(recency_sums[:, t : t + 1], (SUB, LANES))
                        for t in range(ub * cells + k * item_blocks, ub * cells + (k + 1) * item_blocks)
                    ],
                    axis=1,
                )
                for ub in range(USER_BLOCKS)
            ],
            axis=0,
        )

    def stacked(value):
        high, low = split_parts(value)
        return jnp.concatenate([high, low], axis=0).astype(jnp.bfloat16)

    def folded(pair):
        return (pair[:users, :features] + pair[:users, features:]) + (pair[users:, :features] + pair[users:, features:])

    def back(values):
        left = jnp.concatenate([stacked(value) for value in values], axis=1)
        return folded(jnp.dot(left, tall[...], preferred_element_type=jnp.float32))

    right = back([conf_of(k) + count_of(k) for k in range(STEPS)])

    def scores_of(value):
        high, low = split_parts(value)
        left = jnp.concatenate(
            [jnp.concatenate([high, high], axis=1), jnp.concatenate([low, low], axis=1)], axis=0
        ).astype(jnp.bfloat16)
        through = jnp.dot(left[:, :features], base_pair[...], preferred_element_type=jnp.float32)
        scores = []
        for k in range(STEPS):
            both = jnp.dot(left, wide[k], preferred_element_type=jnp.float32)
            scores.append(both[:users] + both[users:])
        return folded(through), scores

    confs = [conf_of(k) for k in range(STEPS)]
    answer = jnp.zeros_like(right)
    residual = right
    direction = right
    norm_now = jnp.sum(residual * residual, axis=1, keepdims=True)
    through, scores = scores_of(right)
    for iteration in range(CG_ITERS):
        weighted = [scores[k] * confs[k] for k in range(STEPS)]
        curve = direction * through
        for k in range(STEPS):
            terms = weighted[k] * scores[k]
            for i in range(item_blocks):
                curve = curve + terms[:, i * LANES : (i + 1) * LANES]
        step = norm_now / jnp.sum(curve, axis=1, keepdims=True)
        answer = answer + step * direction
        if iteration + 1 < CG_ITERS:
            image = through + back(weighted)
            residual = residual - step * image
            norm_next = jnp.sum(residual * residual, axis=1, keepdims=True)
            through_next, scores_next = scores_of(residual)
            ratio = norm_next / norm_now
            direction = residual + ratio * direction
            through = through_next + ratio * through
            scores = [n + ratio * s for n, s in zip(scores_next, scores)]
            norm_now = norm_next
    out[...] = answer


def body(item_emb, confidences, user_block, item_block, block_age, block_count):
    n_item, n_split = lax.axis_size("item"), lax.axis_size("split")
    rows, features = item_emb.shape
    block_users, block_items = confidences.shape[4:]
    item_blocks = rows // block_items
    half = pl.cdiv(USER_BLOCKS * STEPS * item_blocks + 1, 2)
    f32 = jnp.float32
    hbm = pl.BlockSpec(memory_space=pltpu.HBM)
    vmem = pl.BlockSpec(memory_space=pltpu.VMEM)
    params = pltpu.CompilerParams(vmem_limit_bytes=VMEM_LIMIT)
    half_tiles = jax.ShapeDtypeStruct((half, SUB, LANES), f32)

    def pair(value, axis):
        return lax.ppermute(value, axis, [(i, i ^ 1) for i in range(lax.axis_size(axis))])

    def shifted(value, axis, steps):
        count = lax.axis_size(axis)
        return lax.ppermute(value, axis, [(i, (i + steps) % count) for i in range(count)])

    def cost(flops):
        return pl.CostEstimate(flops=flops, bytes_accessed=0, transcendentals=0)

    slot_arrays = (user_block, item_block, block_age, block_count)
    keep, send = pl.pallas_call(
        functools.partial(weights_kernel, item_blocks, half),
        out_shape=[half_tiles, half_tiles],
        in_specs=[hbm] * 5,
        out_specs=[vmem] * 2,
        scratch_shapes=[pltpu.SMEM(a.shape, a.dtype) for a in slot_arrays]
        + [
            pltpu.VMEM(confidences.shape, confidences.dtype),
            pltpu.VMEM((2 * half, SUB, LANES), f32),
            pltpu.SemaphoreType.DMA((5,)),
        ],
        compiler_params=params,
        name="weights",
    )(*[pltpu.with_memory_space_constraint(a, pltpu.HBM) for a in (*slot_arrays, confidences)])
    with jax.named_scope("near_halves"):
        keep = keep + pair(send, "split")

    with jax.named_scope("second_shard"):
        second = shifted(item_emb, "item", 2)
    with jax.named_scope("first_shard"):
        first = lax.ppermute(item_emb, "item", [(i, (i + (3 if i % 2 else 1)) % n_item) for i in range(n_item)])
    total = keep
    with jax.named_scope("far_halves"):
        for steps in range(2, n_split, 2):
            total = total + shifted(keep, "split", steps)
    ready, _ = lax.optimization_barrier((second, keep))
    two_gram = pl.pallas_call(
        gram_kernel,
        out_shape=jax.ShapeDtypeStruct((features, features), f32),
        in_specs=[vmem] * 2,
        out_specs=vmem,
        compiler_params=params,
        name="gram",
    )(item_emb, ready)
    with jax.named_scope("chip_gram"):
        four_gram = two_gram + pair(two_gram, "item")
    with jax.named_scope("all_gram"):
        grams = [shifted(four_gram, "item", steps) for steps in range(STEPS, n_item, STEPS)]
    gram = pl.pallas_call(
        sum_kernel,
        out_shape=jax.ShapeDtypeStruct((features, features), f32),
        in_specs=[vmem] * (1 + len(grams)),
        out_specs=vmem,
        compiler_params=params,
        cost_estimate=cost(SUM_COST),
        name="sum",
    )(four_gram, *grams)
    total, ready = lax.optimization_barrier((total, ready))
    with jax.named_scope("third_shard"):
        third = pair(ready, "item")
    gram, first = lax.optimization_barrier((gram, first))
    with jax.named_scope("other_half"):
        other = pair(total, "split")
    other, gram = lax.optimization_barrier((other, gram))
    low, high = pl.pallas_call(
        place_kernel,
        out_shape=[half_tiles] * 2,
        in_specs=[vmem] * 2,
        out_specs=[vmem] * 2,
        compiler_params=params,
        name="place",
    )(total, other)

    base_pair = pl.pallas_call(
        base_kernel,
        out_shape=jax.ShapeDtypeStruct((features, 2 * features), jnp.bfloat16),
        in_specs=[vmem],
        out_specs=vmem,
        compiler_params=params,
        cost_estimate=cost(BASE_COST),
        name="base",
    )(gram)
    return pl.pallas_call(
        functools.partial(solve_kernel, item_blocks, half),
        out_shape=jax.ShapeDtypeStruct((USER_BLOCKS * block_users, features), f32),
        in_specs=[vmem] * (STEPS + 3),
        out_specs=vmem,
        scratch_shapes=[
            pltpu.VMEM((STEPS, 2 * features, rows), jnp.bfloat16),
            pltpu.VMEM((STEPS * rows, 2 * features), jnp.bfloat16),
        ],
        compiler_params=params,
        name="solve",
    )(item_emb, first, second, third, base_pair, low, high)


def solution(mesh):
    placed = (
        P("item", None),
        P("item", "split", None, None, None, None),
        P("item", "split", None, None),
        P("item", "split", None, None),
        P("item", "split", None, None),
        P("item", "split", None),
    )
    return jax.shard_map(
        body, mesh=mesh, in_specs=placed, out_specs=P("item", None), check_vma=False
    )
```
